32 devices in a mesh: groups: 2 (over y), users: 4 (over z), hours: 4 (over x, core).
Axes of the slice: x: 2, y: 2, z: 4, core: 2. Of those that a mesh axis runs over, the one named last changes fastest.
Arguments:
- activity: bfloat16 [16384, 8192], P(('groups', 'users'), 'hours'), parts along dimension 0, may hold values from -6 to 6
- cohort: int32 [16384], P(('groups', 'users')), parts along dimension 0, may hold values from 0 to 15
- tap_table: float32 [16, 9], replicated, may hold values from 0.02 to 0.4
- sketch: bfloat16 [8192, 64], P('hours'), may hold values from -0.0625 to 0.0625
Outputs:
- basis: float32 [16384, 64], P(('groups', 'users', 'hours')), parts along dimension 0
- triangle: float32 [128, 64], P('groups'), parts along dimension 0
The draws below stay inside these ranges and needn't reach their ends.
There are 2 independent parts, one for each index of `groups`. The reference program is written for one: setup_inputs(seed, part) draws one part's arguments, and reference() takes and returns one part's arrays. A program takes and returns all parts, laid end to end along the dimension named above; an argument that names none is the same for every part. Nothing has to cross between parts.
All inputs are finite; a program needn't handle non-finite values.
Results may differ from the reference program's by a relative error of at most 0.003.
Values may be sent and summed in bfloat16 or wider, within the bound.
A program may use at most 64 MiB of HBM per device.

```python
import jax
import jax.numpy as jnp
from jax import lax

K = 64
TAPS = 9
COHORTS = 16
U_DEV = 2048
U = 8192
H = 8192


def plant(drawn, key, low, largest):
    longest = drawn.shape.index(max(drawn.shape))
    spots = []
    for shift in (0, 1):
        where = [jax.random.randint(jax.random.fold_in(key, axis), (), 0, length) for axis, length in enumerate(drawn.shape)]
        where[longest] = (where[longest] + shift) % drawn.shape[longest]
        spots.append(tuple(where))
    return drawn.at[spots[0]].set(low).at[spots[1]].set(largest)


def block_scale(own_key, dims, shards, smallest, high):
    gain, own = 1.0, jax.random.fold_in(own_key, 6)
    for axis_at, parts in shards:
        heights = jnp.exp(jax.random.uniform(jax.random.fold_in(own, axis_at), (parts,), jnp.float32, smallest / len(shards), high / len(shards)))
        gain = gain * jnp.repeat(heights, dims[axis_at] // parts).reshape([-1 if axis == axis_at else 1 for axis in range(len(dims))])
    return gain


def scatter_about(stream_key, shape, width, limit, shards=(), kind=jnp.bfloat16):
    values = width * jax.random.normal(stream_key, shape, jnp.float32)
    if shards:
        values = values * block_scale(stream_key, shape, shards, -0.22, 0.18)
    return jnp.clip(values, -limit, limit).astype(kind)


def setup_inputs(seed: int = 0, part: int = 0) -> dict:
    key_list = jax.random.split(jax.random.key(seed), 5)
    part_splits = jax.random.split(jax.random.fold_in(key_list[4], part), 5)
    return {
        "activity": scatter_about(part_splits[0], (U, H), 1.0, 6.0, ((0, 4), (1, 4))),
        "cohort": plant(jax.random.randint(part_splits[1], (U,), 0, COHORTS), jax.random.fold_in(part_splits[1], 1), 0, COHORTS - 1).astype(jnp.int32),
        "tap_table": jnp.clip(jax.random.uniform(key_list[2], (COHORTS, TAPS), jnp.float32, 0.02, 0.4), 0.02, 0.4),
        "sketch": scatter_about(key_list[3], (H, K), H ** -0.5, 0.0625, ((0, 4),)),
    }


def smooth_block(rows_in, ids, tap_table, sketch):
    table_width = tap_table.shape[0]
    onehot = (ids[:, None] == jnp.arange(table_width, dtype=jnp.int32)[None, :]).astype(jnp.float32)
    taps = jnp.dot(onehot, tap_table, precision=lax.Precision.HIGHEST)
    reach = (TAPS - 1) // 2
    hours_all = rows_in.shape[1]
    padded = jnp.pad(rows_in, ((0, 0), (reach, reach)))
    total = jnp.zeros(rows_in.shape, jnp.float32)
    for step in range(TAPS):
        total = total + taps[:, step:step + 1] * padded[:, step:step + hours_all].astype(jnp.float32)
    smoothed = total.astype(jnp.bfloat16)
    return jnp.dot(smoothed.astype(jnp.float32), sketch.astype(jnp.float32), preferred_element_type=jnp.float32)

def reference(activity, cohort, tap_table, sketch):
    users_all, hours_all = activity.shape
    blocks = users_all // U_DEV
    stacked = activity.reshape(blocks, U_DEV, hours_all)
    ids = cohort.reshape(blocks, U_DEV)
    projected = lax.map(lambda pair: smooth_block(pair[0], pair[1], tap_table, sketch), (stacked, ids))
    projected = projected.reshape(users_all, sketch.shape[1])
    gram = jnp.dot(projected.T, projected, precision=lax.Precision.HIGHEST)
    lower = jnp.linalg.cholesky(gram)
    basis = lax.linalg.triangular_solve(lower, projected, left_side=False, lower=True, transpose_a=True)
    triangle = lower.T / jnp.sqrt(jnp.float32(users_all))
    return (basis, triangle)
```

```python
import functools
import math

import jax
import jax.numpy as jnp
from jax import lax
from jax.experimental import pallas as pl
from jax.experimental.pallas import tpu as pltpu
from jax.sharding import PartitionSpec as P

TAPS = 9
REACH = (TAPS - 1) // 2
EDGE = 128
HIGHEST = lax.Precision.HIGHEST
MESH = pl.DeviceIdType.MESH


def flip(index, mask):
    bit = 1
    while bit <= mask:
        if mask & bit:
            index = index + bit - 2 * bit * ((index // bit) % 2)
        bit *= 2
    return index


def dot_nt(a, b, precision=None):
    return lax.dot_general(
        a, b, (((1,), (1,)), ((), ())), precision=precision, preferred_element_type=jnp.float32
    )


def eliminate(gram):
    k = gram.shape[0]
    row_id = lax.broadcasted_iota(jnp.int32, (k, 2 * k), 0)
    lane_id = lax.broadcasted_iota(jnp.int32, (k, 2 * k), 1)
    eye = (row_id[:, :k] == lane_id[:, :k]).astype(jnp.float32)
    work = jnp.concatenate([gram, eye], axis=1)
    for step in range(k - 1):
        row = work[step : step + 1, :]
        scaled = row / work[step : step + 1, step : step + 1]
        col = jnp.where(row_id > step, work[:, step : step + 1], 0.0)
        work = work - col * scaled
    diag = jnp.sum(jnp.where(row_id == lane_id, work, 0.0), axis=1, keepdims=True)
    work = work * lax.rsqrt(diag)
    upper = jnp.where(row_id[:, :k] <= lane_id[:, :k], work[:, :k], 0.0)
    inverse = jnp.where(row_id[:, :k] >= lane_id[:, :k], work[:, k:], 0.0)
    return upper, inverse


def pack(square):
    half = square.shape[0] // 2
    return jnp.concatenate([square[:half], square[half:]], axis=1)


def unpack(packed):
    k = packed.shape[1] // 2
    return jnp.concatenate([packed[:, :k], packed[:, k:]], axis=0)


def kernel(
    n_users, n_hours, activity, cohort, table, sketch, basis, triangle,
    block, edge, shifted, taps, send, recv, gram_h, gram_u,
    load_sem, edge_send, edge_recv, part_send, part_recv, gh_send, gh_recv, gu_send, gu_recv,
):
    users = lax.axis_index("users")
    hours = lax.axis_index("hours")
    rows, width = activity.shape
    k = sketch.shape[0]
    share = rows // n_hours

    order = list(range(n_hours - 1, 0, -1)) + [0]
    loads = []
    for mask in order:
        start = pl.multiple_of(flip(hours, mask) * share, share)
        load = pltpu.make_async_copy(
            activity.at[pl.ds(start, share), :], block.at[mask], load_sem.at[mask]
        )
        load.start()
        loads.append(load)

    barrier = pltpu.get_barrier_semaphore()
    for mask in range(1, n_hours):
        pl.semaphore_signal(
            barrier, inc=1, device_id={"hours": flip(hours, mask)}, device_id_type=MESH
        )
    for step in range(1, n_users):
        pl.semaphore_signal(
            barrier, inc=1, device_id={"users": (users + step) % n_users}, device_id_type=MESH
        )
    pl.semaphore_wait(barrier, n_hours - 1 + n_users - 1)

    to_right = pltpu.make_async_remote_copy(
        src_ref=sketch.at[:, pl.ds(width - EDGE, EDGE)],
        dst_ref=edge.at[0],
        send_sem=edge_send.at[0],
        recv_sem=edge_recv.at[0],
        device_id={"hours": (hours + 1) % n_hours},
        device_id_type=MESH,
    )
    to_left = pltpu.make_async_remote_copy(
        src_ref=sketch.at[:, pl.ds(0, EDGE)],
        dst_ref=edge.at[1],
        send_sem=edge_send.at[1],
        recv_sem=edge_recv.at[1],
        device_id={"hours": (hours + n_hours - 1) % n_hours},
        device_id_type=MESH,
    )
    to_right.start()
    to_left.start()

    cohorts = table.shape[0]
    onehot = (
        lax.broadcasted_iota(jnp.int32, (cohorts, rows), 0) == cohort[...]
    ).astype(jnp.float32)
    taps[...] = lax.dot_general(
        table[...], onehot, (((0,), (0,)), ((), ())),
        precision=HIGHEST, preferred_element_type=jnp.float32,
    )

    to_right.wait()
    to_left.wait()
    low = edge[0].astype(jnp.float32)
    high = edge[1].astype(jnp.float32)
    turned = jnp.concatenate(
        [
            jnp.where(hours > 0, low, jnp.zeros_like(low)),
            sketch[...].astype(jnp.float32),
            jnp.where(hours < n_hours - 1, high, jnp.zeros_like(high)),
        ],
        axis=1,
    )
    for step in range(TAPS):
        shift = (step - REACH) % turned.shape[1]
        moved = turned if shift == 0 else pltpu.roll(turned, shift, 1)
        shifted[pl.ds(step * k, k), :] = moved[:, EDGE : EDGE + width].astype(jnp.bfloat16)

    parts = []
    local = None
    for load, mask in zip(loads, order):
        load.wait()
        start = pl.multiple_of(flip(hours, mask) * share, share)
        product = dot_nt(shifted[...], block[mask])
        total = taps[pl.ds(0, 1), pl.ds(start, share)] * product[:k]
        for step in range(1, TAPS):
            total += (
                taps[pl.ds(step, 1), pl.ds(start, share)] * product[step * k : (step + 1) * k]
            )
        if mask:
            send[mask - 1] = total
            copy = pltpu.make_async_remote_copy(
                src_ref=send.at[mask - 1],
                dst_ref=recv.at[mask - 1],
                send_sem=part_send.at[mask - 1],
                recv_sem=part_recv.at[mask - 1],
                device_id={"hours": flip(hours, mask)},
                device_id_type=MESH,
            )
            copy.start()
            parts.append((copy, mask))
        else:
            local = total
    for copy, mask in reversed(parts):
        copy.wait()
        local = local + recv[mask - 1]

    gram = pack(dot_nt(local, local, HIGHEST))
    for axis, count, me, slots, send_sems, recv_sems in (
        ("hours", n_hours, hours, gram_h, gh_send, gh_recv),
        ("users", n_users, users, gram_u, gu_send, gu_recv),
    ):
        slots[me] = gram
        copies = []
        for step in range(1, count):
            copy = pltpu.make_async_remote_copy(
                src_ref=slots.at[me],
                dst_ref=slots.at[me],
                send_sem=send_sems.at[step - 1],
                recv_sem=recv_sems.at[step - 1],
                device_id={axis: (me + step) % count},
                device_id_type=MESH,
            )
            copy.start()
            copies.append(copy)
        for copy in copies:
            copy.wait()
        gram = slots[0]
        for slot in range(1, count):
            gram = gram + slots[slot]

    upper, inverse = eliminate(unpack(gram))
    triangle[...] = upper * (1.0 / math.sqrt(rows * n_users))
    basis[...] = jnp.dot(
        inverse, local, precision=HIGHEST, preferred_element_type=jnp.float32
    )


def per_device(activity, cohort, tap_table, sketch):
    n_users, n_hours = lax.axis_size("users"), lax.axis_size("hours")
    rows, width = activity.shape
    k = sketch.shape[1]
    share = rows // n_hours
    dma = lambda count: pltpu.SemaphoreType.DMA((count,))
    vmem = pl.BlockSpec(memory_space=pltpu.VMEM)
    basis, triangle = pl.pallas_call(
        functools.partial(kernel, n_users, n_hours),
        out_shape=(
            jax.ShapeDtypeStruct((k, share), jnp.float32),
            jax.ShapeDtypeStruct((k, k), jnp.float32),
        ),
        in_specs=[pl.BlockSpec(memory_space=pl.ANY), vmem, vmem, vmem],
        out_specs=(vmem, vmem),
        scratch_shapes=[
            pltpu.VMEM((n_hours, share, width), jnp.bfloat16),
            pltpu.VMEM((2, k, EDGE), jnp.bfloat16),
            pltpu.VMEM((TAPS * k, width), jnp.bfloat16),
            pltpu.VMEM((TAPS, rows), jnp.float32),
            pltpu.VMEM((n_hours - 1, k, share), jnp.float32),
            pltpu.VMEM((n_hours - 1, k, share), jnp.float32),
            pltpu.VMEM((n_hours, k // 2, 2 * k), jnp.float32),
            pltpu.VMEM((n_users, k // 2, 2 * k), jnp.float32),
            dma(n_hours), dma(2), dma(2),
            dma(n_hours - 1), dma(n_hours - 1),
            dma(n_hours - 1), dma(n_hours - 1),
            dma(n_users - 1), dma(n_users - 1),
        ],
        compiler_params=pltpu.CompilerParams(
            collective_id=0, has_side_effects=True, vmem_limit_bytes=56 * 1024 * 1024
        ),
        name="range_finder",
    )(activity, cohort[None, :], tap_table, sketch.T)
    return basis.T, triangle


def solution(mesh):
    return jax.shard_map(
        per_device,
        mesh=mesh,
        in_specs=(P(("groups", "users"), "hours"), P(("groups", "users")), P(), P("hours", None)),
        out_specs=(P(("groups", "users", "hours"), None), P("groups", None)),
        check_vma=False,
    )
```

```python
import functools
import math

import jax
import jax.numpy as jnp
from jax import lax
from jax.experimental import pallas as pl
from jax.experimental.pallas import tpu as pltpu
from jax.sharding import PartitionSpec as P

TAPS = 9
REACH = (TAPS - 1) // 2
EDGE = 128
PANEL = 8
HIGHEST = lax.Precision.HIGHEST
MESH = pl.DeviceIdType.MESH


def flip(index, mask):
    bit = 1
    while bit <= mask:
        if mask & bit:
            index = index + bit - 2 * bit * ((index // bit) % 2)
        bit *= 2
    return index


def dot_nt(a, b, precision=None):
    return lax.dot_general(
        a, b, (((1,), (1,)), ((), ())), precision=precision, preferred_element_type=jnp.float32
    )


def eliminate(gram):
    k = gram.shape[0]
    row_id = lax.broadcasted_iota(jnp.int32, (k, 2 * k), 0)
    lane_id = lax.broadcasted_iota(jnp.int32, (k, 2 * k), 1)
    eye = (row_id[:, :k] == lane_id[:, :k]).astype(jnp.float32)
    work = jnp.concatenate([gram, eye], axis=1)
    diag_id = lax.broadcasted_iota(jnp.int32, (PANEL, 2 * k), 0)
    done = []
    for first in range(0, k, PANEL):
        rows = work.shape[0]
        below = lax.broadcasted_iota(jnp.int32, (rows, 2 * k), 0)
        cols = [
            jnp.broadcast_to(work[:, first + i : first + i + 1], (rows, 2 * k))
            for i in range(PANEL)
        ]
        pivots = jnp.zeros((PANEL, 2 * k), jnp.float32)
        for i in range(PANEL):
            pivot = cols[i][i : i + 1, :]
            pivots = jnp.where(diag_id == i, pivot, pivots)
            col = jnp.where(below > i, cols[i], 0.0) * (1.0 / pivot)
            for later in range(i + 1, PANEL):
                cols[later] = cols[later] - col * cols[i][later : later + 1, :]
            work = work - col * work[i : i + 1, :]
        done.append(work[:PANEL] * lax.rsqrt(pivots))
        work = work[PANEL:]
    work = jnp.concatenate(done, axis=0)
    upper = jnp.where(row_id[:, :k] <= lane_id[:, :k], work[:, :k], 0.0)
    inverse = jnp.where(row_id[:, :k] >= lane_id[:, :k], work[:, k:], 0.0)
    return upper, inverse


def pack(square):
    half = square.shape[0] // 2
    return jnp.concatenate([square[:half], square[half:]], axis=1)


def unpack(packed):
    k = packed.shape[1] // 2
    return jnp.concatenate([packed[:, :k], packed[:, k:]], axis=0)


def kernel(
    n_users, n_hours, activity, cohort, table, sketch, local_out, gram_out,
    block, edge, shifted, ends, taps, send, recv, gram_h, gram_u,
    load_sem, edge_send, edge_recv, part_send, part_recv, gh_send, gh_recv, gu_send, gu_recv,
):
    users = lax.axis_index("users")
    hours = lax.axis_index("hours")
    rows, width = activity.shape
    k = sketch.shape[0]
    share = rows // n_hours

    order = list(range(n_hours - 1, 0, -1)) + [0]
    loads = []
    for mask in order:
        start = pl.multiple_of(flip(hours, mask) * share, share)
        load = pltpu.make_async_copy(
            activity.at[pl.ds(start, share), :], block.at[mask], load_sem.at[mask]
        )
        load.start()
        loads.append(load)

    barrier = pltpu.get_barrier_semaphore()
    for mask in range(1, n_hours):
        pl.semaphore_signal(
            barrier, inc=1, device_id={"hours": flip(hours, mask)}, device_id_type=MESH
        )
    for step in range(1, n_users):
        pl.semaphore_signal(
            barrier, inc=1, device_id={"users": (users + step) % n_users}, device_id_type=MESH
        )
    pl.semaphore_wait(barrier, n_hours - 1 + n_users - 1)

    to_right = pltpu.make_async_remote_copy(
        src_ref=sketch.at[:, pl.ds(width - EDGE, EDGE)],
        dst_ref=edge.at[0],
        send_sem=edge_send.at[0],
        recv_sem=edge_recv.at[0],
        device_id={"hours": (hours + 1) % n_hours},
        device_id_type=MESH,
    )
    to_left = pltpu.make_async_remote_copy(
        src_ref=sketch.at[:, pl.ds(0, EDGE)],
        dst_ref=edge.at[1],
        send_sem=edge_send.at[1],
        recv_sem=edge_recv.at[1],
        device_id={"hours": (hours + n_hours - 1) % n_hours},
        device_id_type=MESH,
    )
    to_right.start()
    to_left.start()

    cohorts = table.shape[0]
    onehot = (
        lax.broadcasted_iota(jnp.int32, (cohorts, rows), 0) == cohort[...]
    ).astype(jnp.float32)
    taps[...] = lax.dot_general(
        table[...], onehot, (((0,), (0,)), ((), ())),
        precision=HIGHEST, preferred_element_type=jnp.float32,
    )

    middle = sketch[...].astype(jnp.float32)
    blank = jnp.zeros((k, EDGE), jnp.float32)
    turned = jnp.concatenate([blank, middle, blank], axis=1)
    for step in range(TAPS):
        shift = (step - REACH) % turned.shape[1]
        moved = turned if shift == 0 else pltpu.roll(turned, shift, 1)
        shifted[pl.ds(step * k, k), :] = moved[:, EDGE : EDGE + width].astype(jnp.bfloat16)

    loads[0].wait()
    product = dot_nt(shifted[...], block[order[0]])

    to_right.wait()
    to_left.wait()
    low = jnp.where(hours > 0, edge[0].astype(jnp.float32), blank)
    high = jnp.where(hours < n_hours - 1, edge[1].astype(jnp.float32), blank)
    turned = jnp.concatenate([low, blank, blank, high], axis=1)
    for step in range(TAPS):
        shift = (step - REACH) % turned.shape[1]
        moved = turned if shift == 0 else pltpu.roll(turned, shift, 1)
        ends[pl.ds(step * k, k), :] = moved[:, EDGE : 3 * EDGE].astype(jnp.bfloat16)
    shifted[:, pl.ds(0, EDGE)] += ends[:, pl.ds(0, EDGE)]
    shifted[:, pl.ds(width - EDGE, EDGE)] += ends[:, pl.ds(EDGE, EDGE)]
    outer = jnp.concatenate(
        [block[order[0], :, pl.ds(0, EDGE)], block[order[0], :, pl.ds(width - EDGE, EDGE)]], axis=1
    )
    product += dot_nt(ends[...], outer)

    copies = {}
    for load, mask in zip(loads, order):
        start = pl.multiple_of(flip(hours, mask) * share, share)
        if mask != order[0]:
            load.wait()
            product = dot_nt(shifted[...], block[mask])
        total = taps[pl.ds(0, 1), pl.ds(start, share)] * product[:k]
        for step in range(1, TAPS):
            total += (
                taps[pl.ds(step, 1), pl.ds(start, share)] * product[step * k : (step + 1) * k]
            )
        bit = 1
        while mask + bit < n_hours and (mask == 0 or bit < mask & -mask):
            copies[mask + bit].wait()
            total += recv[mask + bit - 1]
            bit *= 2
        if mask:
            send[mask - 1] = total
            copies[mask] = pltpu.make_async_remote_copy(
                src_ref=send.at[mask - 1],
                dst_ref=recv.at[mask - 1],
                send_sem=part_send.at[mask - 1],
                recv_sem=part_recv.at[mask - 1],
                device_id={"hours": flip(hours, mask & -mask)},
                device_id_type=MESH,
            )
            copies[mask].start()
    local = total
    local_out[...] = local

    gram = pack(dot_nt(local, local, HIGHEST))
    for axis, count, me, slots, send_sems, recv_sems in (
        ("hours", n_hours, hours, gram_h, gh_send, gh_recv),
        ("users", n_users, users, gram_u, gu_send, gu_recv),
    ):
        slots[me] = gram
        copies = []
        for step in range(1, count):
            copy = pltpu.make_async_remote_copy(
                src_ref=slots.at[me],
                dst_ref=slots.at[me],
                send_sem=send_sems.at[step - 1],
                recv_sem=recv_sems.at[step - 1],
                device_id={axis: (me + step) % count},
                device_id_type=MESH,
            )
            copy.start()
            copies.append(copy)
        for copy in copies:
            copy.wait()
        gram = slots[0]
        for slot in range(1, count):
            gram = gram + slots[slot]

    gram_out[...] = gram


def finish(scale, local, gram, basis, triangle):
    upper, inverse = eliminate(unpack(gram[...]))
    triangle[...] = upper * scale
    basis[...] = jnp.dot(
        inverse, local[...], precision=HIGHEST, preferred_element_type=jnp.float32
    )


def per_device(activity, cohort, tap_table, sketch):
    n_users, n_hours = lax.axis_size("users"), lax.axis_size("hours")
    rows, width = activity.shape
    k = sketch.shape[1]
    share = rows // n_hours
    dma = lambda count: pltpu.SemaphoreType.DMA((count,))
    vmem = pl.BlockSpec(memory_space=pltpu.VMEM)
    local, gram = pl.pallas_call(
        functools.partial(kernel, n_users, n_hours),
        out_shape=(
            jax.ShapeDtypeStruct((k, share), jnp.float32),
            jax.ShapeDtypeStruct((k // 2, 2 * k), jnp.float32),
        ),
        in_specs=[pl.BlockSpec(memory_space=pl.ANY), vmem, vmem, vmem],
        out_specs=(vmem, vmem),
        scratch_shapes=[
            pltpu.VMEM((n_hours, share, width), jnp.bfloat16),
            pltpu.VMEM((2, k, EDGE), jnp.bfloat16),
            pltpu.VMEM((TAPS * k, width), jnp.bfloat16),
            pltpu.VMEM((TAPS * k, 2 * EDGE), jnp.bfloat16),
            pltpu.VMEM((TAPS, rows), jnp.float32),
            pltpu.VMEM((n_hours - 1, k, share), jnp.float32),
            pltpu.VMEM((n_hours - 1, k, share), jnp.float32),
            pltpu.VMEM((n_hours, k // 2, 2 * k), jnp.float32),
            pltpu.VMEM((n_users, k // 2, 2 * k), jnp.float32),
            dma(n_hours), dma(2), dma(2),
            dma(n_hours - 1), dma(n_hours - 1),
            dma(n_hours - 1), dma(n_hours - 1),
            dma(n_users - 1), dma(n_users - 1),
        ],
        compiler_params=pltpu.CompilerParams(
            collective_id=0, has_side_effects=True, vmem_limit_bytes=56 * 1024 * 1024
        ),
        name="range_finder",
    )(activity, cohort[None, :], tap_table, sketch.T)
    basis, triangle = pl.pallas_call(
        functools.partial(finish, 1.0 / math.sqrt(rows * n_users)),
        out_shape=(
            jax.ShapeDtypeStruct((k, share), jnp.float32),
            jax.ShapeDtypeStruct((k, k), jnp.float32),
        ),
        in_specs=[vmem, vmem],
        out_specs=(vmem, vmem),
        name="factor",
    )(local, gram)
    return basis.T, triangle


def solution(mesh):
    return jax.shard_map(
        per_device,
        mesh=mesh,
        in_specs=(P(("groups", "users"), "hours"), P(("groups", "users")), P(), P("hours", None)),
        out_specs=(P(("groups", "users", "hours"), None), P("groups", None)),
        check_vma=False,
    )
```

```python
import functools
import math

import jax
import jax.numpy as jnp
from jax import lax
from jax.experimental import pallas as pl
from jax.experimental.pallas import tpu as pltpu
from jax.sharding import PartitionSpec as P

TAPS = 9
REACH = (TAPS - 1) // 2
EDGE = 128
PANEL = 8
HIGHEST = lax.Precision.HIGHEST
MESH = pl.DeviceIdType.MESH


def flip(index, mask):
    bit = 1
    while bit <= mask:
        if mask & bit:
            index = index + bit - 2 * bit * ((index // bit) % 2)
        bit *= 2
    return index


def dot_nt(a, b, precision=None):
    return lax.dot_general(
        a, b, (((1,), (1,)), ((), ())), precision=precision, preferred_element_type=jnp.float32
    )


def multiply(shifted, block, slot):
    share = block.shape[1]
    half = share // 2
    return jnp.concatenate(
        [dot_nt(shifted[...], block[slot, pl.ds(first, half), :]) for first in (0, half)], axis=1
    )


def eliminate(gram):
    k = gram.shape[0]
    row_id = lax.broadcasted_iota(jnp.int32, (k, 2 * k), 0)
    lane_id = lax.broadcasted_iota(jnp.int32, (k, 2 * k), 1)
    eye = (row_id[:, :k] == lane_id[:, :k]).astype(jnp.float32)
    work = jnp.concatenate([gram, eye], axis=1)
    diag_id = lax.broadcasted_iota(jnp.int32, (PANEL, 2 * k), 0)
    done = []
    for first in range(0, k, PANEL):
        rows = work.shape[0]
        below = lax.broadcasted_iota(jnp.int32, (rows, 2 * k), 0)
        cols = [
            jnp.broadcast_to(work[:, first + i : first + i + 1], (rows, 2 * k))
            for i in range(PANEL)
        ]
        pivots = jnp.zeros((PANEL, 2 * k), jnp.float32)
        for i in range(PANEL):
            pivot = cols[i][i : i + 1, :]
            pivots = jnp.where(diag_id == i, pivot, pivots)
            col = jnp.where(below > i, cols[i], 0.0) * (1.0 / pivot)
            for later in range(i + 1, PANEL):
                cols[later] = cols[later] - col * cols[i][later : later + 1, :]
            work = work - col * work[i : i + 1, :]
        done.append(work[:PANEL] * lax.rsqrt(pivots))
        work = work[PANEL:]
    work = jnp.concatenate(done, axis=0)
    upper = jnp.where(row_id[:, :k] <= lane_id[:, :k], work[:, :k], 0.0)
    inverse = jnp.where(row_id[:, :k] >= lane_id[:, :k], work[:, k:], 0.0)
    return upper, inverse


def pack(square):
    half = square.shape[0] // 2
    return jnp.concatenate([square[:half], square[half:]], axis=1)


def unpack(packed):
    k = packed.shape[1] // 2
    return jnp.concatenate([packed[:, :k], packed[:, k:]], axis=0)


def kernel(
    n_users, n_hours, activity, cohort, table, sketch, local_out, gram_out,
    block, edge, shifted, ends, taps, send, recv, gram_h, gram_u,
    load_sem, edge_send, edge_recv, part_send, part_recv, gh_send, gh_recv, gu_send, gu_recv,
):
    users = lax.axis_index("users")
    hours = lax.axis_index("hours")
    rows, width = activity.shape
    k = sketch.shape[0]
    share = rows // n_hours

    order = list(range(n_hours - 1, 0, -1)) + [0]
    loads = []
    for mask in order:
        start = pl.multiple_of(flip(hours, mask) * share, share)
        load = pltpu.make_async_copy(
            activity.at[pl.ds(start, share), :], block.at[mask], load_sem.at[mask]
        )
        load.start()
        loads.append(load)

    barrier = pltpu.get_barrier_semaphore()
    for mask in range(1, n_hours):
        pl.semaphore_signal(
            barrier, inc=1, device_id={"hours": flip(hours, mask)}, device_id_type=MESH
        )
    for step in range(1, n_users):
        pl.semaphore_signal(
            barrier, inc=1, device_id={"users": (users + step) % n_users}, device_id_type=MESH
        )
    cohorts = table.shape[0]
    onehot = (
        lax.broadcasted_iota(jnp.int32, (cohorts, rows), 0) == cohort[...]
    ).astype(jnp.float32)
    taps[...] = lax.dot_general(
        table[...], onehot, (((0,), (0,)), ((), ())),
        precision=HIGHEST, preferred_element_type=jnp.float32,
    )

    middle = sketch[...].astype(jnp.float32)
    blank = jnp.zeros((k, EDGE), jnp.float32)
    turned = jnp.concatenate([blank, middle, blank], axis=1)
    for step in range(TAPS):
        shift = (step - REACH) % turned.shape[1]
        moved = turned if shift == 0 else pltpu.roll(turned, shift, 1)
        shifted[pl.ds(step * k, k), :] = moved[:, EDGE : EDGE + width].astype(jnp.bfloat16)

    pl.semaphore_wait(barrier, n_hours - 1 + n_users - 1)

    to_right = pltpu.make_async_remote_copy(
        src_ref=sketch.at[:, pl.ds(width - EDGE, EDGE)],
        dst_ref=edge.at[0],
        send_sem=edge_send.at[0],
        recv_sem=edge_recv.at[0],
        device_id={"hours": (hours + 1) % n_hours},
        device_id_type=MESH,
    )
    to_left = pltpu.make_async_remote_copy(
        src_ref=sketch.at[:, pl.ds(0, EDGE)],
        dst_ref=edge.at[1],
        send_sem=edge_send.at[1],
        recv_sem=edge_recv.at[1],
        device_id={"hours": (hours + n_hours - 1) % n_hours},
        device_id_type=MESH,
    )
    to_right.start()
    to_left.start()

    loads[0].wait()
    product = multiply(shifted, block, order[0])

    to_right.wait()
    to_left.wait()
    low = jnp.where(hours > 0, edge[0].astype(jnp.float32), blank)
    high = jnp.where(hours < n_hours - 1, edge[1].astype(jnp.float32), blank)
    turned = jnp.concatenate([low, blank, blank, high], axis=1)
    for step in range(TAPS):
        shift = (step - REACH) % turned.shape[1]
        moved = turned if shift == 0 else pltpu.roll(turned, shift, 1)
        ends[pl.ds(step * k, k), :] = moved[:, EDGE : 3 * EDGE].astype(jnp.bfloat16)
    shifted[:, pl.ds(0, EDGE)] += ends[:, pl.ds(0, EDGE)]
    shifted[:, pl.ds(width - EDGE, EDGE)] += ends[:, pl.ds(EDGE, EDGE)]
    outer = jnp.concatenate(
        [block[order[0], :, pl.ds(0, EDGE)], block[order[0], :, pl.ds(width - EDGE, EDGE)]], axis=1
    )
    product += dot_nt(ends[...], outer)

    copies = {}
    for load, mask in zip(loads, order):
        start = pl.multiple_of(flip(hours, mask) * share, share)
        if mask != order[0]:
            load.wait()
            product = multiply(shifted, block, mask)
        total = taps[pl.ds(0, 1), pl.ds(start, share)] * product[:k]
        for step in range(1, TAPS):
            total += (
                taps[pl.ds(step, 1), pl.ds(start, share)] * product[step * k : (step + 1) * k]
            )
        bit = 1
        while mask + bit < n_hours and (mask == 0 or bit < mask & -mask):
            copies[mask + bit].wait()
            total += recv[mask + bit - 1]
            bit *= 2
        if mask:
            send[mask - 1] = total
            copies[mask] = pltpu.make_async_remote_copy(
                src_ref=send.at[mask - 1],
                dst_ref=recv.at[mask - 1],
                send_sem=part_send.at[mask - 1],
                recv_sem=part_recv.at[mask - 1],
                device_id={"hours": flip(hours, mask & -mask)},
                device_id_type=MESH,
            )
            copies[mask].start()
    local = total
    local_out[...] = local

    gram = pack(dot_nt(local, local, HIGHEST))
    for axis, count, me, slots, send_sems, recv_sems in (
        ("hours", n_hours, hours, gram_h, gh_send, gh_recv),
        ("users", n_users, users, gram_u, gu_send, gu_recv),
    ):
        slots[me] = gram
        copies = []
        for step in range(1, count):
            copy = pltpu.make_async_remote_copy(
                src_ref=slots.at[me],
                dst_ref=slots.at[me],
                send_sem=send_sems.at[step - 1],
                recv_sem=recv_sems.at[step - 1],
                device_id={axis: (me + step) % count},
                device_id_type=MESH,
            )
            copy.start()
            copies.append(copy)
        for copy in copies:
            copy.wait()
        gram = slots[0]
        for slot in range(1, count):
            gram = gram + slots[slot]

    gram_out[...] = gram


def finish(scale, local, gram, basis, triangle):
    upper, inverse = eliminate(unpack(gram[...]))
    triangle[...] = upper * scale
    basis[...] = jnp.dot(
        inverse, local[...], precision=HIGHEST, preferred_element_type=jnp.float32
    )


def per_device(activity, cohort, tap_table, sketch):
    n_users, n_hours = lax.axis_size("users"), lax.axis_size("hours")
    rows, width = activity.shape
    k = sketch.shape[1]
    share = rows // n_hours
    dma = lambda count: pltpu.SemaphoreType.DMA((count,))
    vmem = pl.BlockSpec(memory_space=pltpu.VMEM)
    local, gram = pl.pallas_call(
        functools.partial(kernel, n_users, n_hours),
        out_shape=(
            jax.ShapeDtypeStruct((k, share), jnp.float32),
            jax.ShapeDtypeStruct((k // 2, 2 * k), jnp.float32),
        ),
        in_specs=[pl.BlockSpec(memory_space=pl.ANY), vmem, vmem, vmem],
        out_specs=(vmem, vmem),
        scratch_shapes=[
            pltpu.VMEM((n_hours, share, width), jnp.bfloat16),
            pltpu.VMEM((2, k, EDGE), jnp.bfloat16),
            pltpu.VMEM((TAPS * k, width), jnp.bfloat16),
            pltpu.VMEM((TAPS * k, 2 * EDGE), jnp.bfloat16),
            pltpu.VMEM((TAPS, rows), jnp.float32),
            pltpu.VMEM((n_hours - 1, k, share), jnp.float32),
            pltpu.VMEM((n_hours - 1, k, share), jnp.float32),
            pltpu.VMEM((n_hours, k // 2, 2 * k), jnp.float32),
            pltpu.VMEM((n_users, k // 2, 2 * k), jnp.float32),
            dma(n_hours), dma(2), dma(2),
            dma(n_hours - 1), dma(n_hours - 1),
            dma(n_hours - 1), dma(n_hours - 1),
            dma(n_users - 1), dma(n_users - 1),
        ],
        compiler_params=pltpu.CompilerParams(
            collective_id=0, has_side_effects=True, vmem_limit_bytes=56 * 1024 * 1024
        ),
        name="range_finder",
    )(activity, cohort[None, :], tap_table, sketch.T)
    basis, triangle = pl.pallas_call(
        functools.partial(finish, 1.0 / math.sqrt(rows * n_users)),
        out_shape=(
            jax.ShapeDtypeStruct((k, share), jnp.float32),
            jax.ShapeDtypeStruct((k, k), jnp.float32),
        ),
        in_specs=[vmem, vmem],
        out_specs=(vmem, vmem),
        name="factor",
    )(local, gram)
    return basis.T, triangle


def solution(mesh):
    return jax.shard_map(
        per_device,
        mesh=mesh,
        in_specs=(P(("groups", "users"), "hours"), P(("groups", "users")), P(), P("hours", None)),
        out_specs=(P(("groups", "users", "hours"), None), P("groups", None)),
        check_vma=False,
    )
```

```python
import functools
import math

import jax
import jax.numpy as jnp
from jax import lax
from jax.experimental import pallas as pl
from jax.experimental.pallas import tpu as pltpu
from jax.sharding import PartitionSpec as P

TAPS = 9
REACH = (TAPS - 1) // 2
EDGE = 128
PANEL = 8
HIGHEST = lax.Precision.HIGHEST
MESH = pl.DeviceIdType.MESH


def flip(index, mask):
    bit = 1
    while bit <= mask:
        if mask & bit:
            index = index + bit - 2 * bit * ((index // bit) % 2)
        bit *= 2
    return index


def dot_nt(a, b, precision=None):
    return lax.dot_general(
        a, b, (((1,), (1,)), ((), ())), precision=precision, preferred_element_type=jnp.float32
    )


def multiply(shifted, block, slot):
    share = block.shape[1]
    half = share // 2
    return jnp.concatenate(
        [dot_nt(shifted[...], block[slot, pl.ds(first, half), :]) for first in (0, half)], axis=1
    )


def eliminate(gram):
    k = gram.shape[0]
    row_id = lax.broadcasted_iota(jnp.int32, (k, 2 * k), 0)
    lane_id = lax.broadcasted_iota(jnp.int32, (k, 2 * k), 1)
    eye = (row_id[:, :k] == lane_id[:, :k]).astype(jnp.float32)
    work = jnp.concatenate([gram, eye], axis=1)
    diag_id = lax.broadcasted_iota(jnp.int32, (PANEL, 2 * k), 0)
    done = []
    for first in range(0, k, PANEL):
        rows = work.shape[0]
        below = lax.broadcasted_iota(jnp.int32, (rows, 2 * k), 0)
        cols = [
            jnp.broadcast_to(work[:, first + i : first + i + 1], (rows, 2 * k))
            for i in range(PANEL)
        ]
        pivots = jnp.zeros((PANEL, 2 * k), jnp.float32)
        for i in range(PANEL):
            pivot = cols[i][i : i + 1, :]
            pivots = jnp.where(diag_id == i, pivot, pivots)
            col = jnp.where(below > i, cols[i], 0.0) * (1.0 / pivot)
            for later in range(i + 1, PANEL):
                cols[later] = cols[later] - col * cols[i][later : later + 1, :]
            work = work - col * work[i : i + 1, :]
        done.append(work[:PANEL] * lax.rsqrt(pivots))
        work = work[PANEL:]
    work = jnp.concatenate(done, axis=0)
    upper = jnp.where(row_id[:, :k] <= lane_id[:, :k], work[:, :k], 0.0)
    inverse = jnp.where(row_id[:, :k] >= lane_id[:, :k], work[:, k:], 0.0)
    return upper, inverse


def pack(square):
    half = square.shape[0] // 2
    return jnp.concatenate([square[:half], square[half:]], axis=1)


def unpack(packed):
    k = packed.shape[1] // 2
    return jnp.concatenate([packed[:, :k], packed[:, k:]], axis=0)


def kernel(
    n_users, n_hours, activity, cohort, table, sketch, local_out, gram_out,
    block, edge, shifted, ends, taps, send, recv, send_far, recv_far, gram_h, gram_u,
    load_sem, edge_send, edge_recv, part_send, part_recv, gh_send, gh_recv, gu_send, gu_recv,
):
    users = lax.axis_index("users")
    hours = lax.axis_index("hours")
    rows, width = activity.shape
    k = sketch.shape[0]
    share = rows // n_hours

    order = list(range(n_hours - 1, 0, -1)) + [0]
    loads = []
    for mask in order:
        start = pl.multiple_of(flip(hours, mask) * share, share)
        load = pltpu.make_async_copy(
            activity.at[pl.ds(start, share), :], block.at[mask], load_sem.at[mask]
        )
        load.start()
        loads.append(load)

    barrier = pltpu.get_barrier_semaphore()
    for mask in range(1, n_hours):
        pl.semaphore_signal(
            barrier, inc=1, device_id={"hours": flip(hours, mask)}, device_id_type=MESH
        )
    for step in range(1, n_users):
        pl.semaphore_signal(
            barrier, inc=1, device_id={"users": (users + step) % n_users}, device_id_type=MESH
        )
    cohorts = table.shape[0]
    onehot = (
        lax.broadcasted_iota(jnp.int32, (cohorts, rows), 0) == cohort[...]
    ).astype(jnp.float32)
    taps[...] = lax.dot_general(
        table[...], onehot, (((0,), (0,)), ((), ())),
        precision=HIGHEST, preferred_element_type=jnp.float32,
    )

    middle = sketch[...].astype(jnp.float32)
    blank = jnp.zeros((k, EDGE), jnp.float32)
    turned = jnp.concatenate([blank, middle, blank], axis=1)
    for step in range(TAPS):
        shift = (step - REACH) % turned.shape[1]
        moved = turned if shift == 0 else pltpu.roll(turned, shift, 1)
        shifted[pl.ds(step * k, k), :] = moved[:, EDGE : EDGE + width].astype(jnp.bfloat16)

    pl.semaphore_wait(barrier, n_hours - 1 + n_users - 1)

    to_right = pltpu.make_async_remote_copy(
        src_ref=sketch.at[:, pl.ds(width - EDGE, EDGE)],
        dst_ref=edge.at[0],
        send_sem=edge_send.at[0],
        recv_sem=edge_recv.at[0],
        device_id={"hours": (hours + 1) % n_hours},
        device_id_type=MESH,
    )
    to_left = pltpu.make_async_remote_copy(
        src_ref=sketch.at[:, pl.ds(0, EDGE)],
        dst_ref=edge.at[1],
        send_sem=edge_send.at[1],
        recv_sem=edge_recv.at[1],
        device_id={"hours": (hours + n_hours - 1) % n_hours},
        device_id_type=MESH,
    )
    to_right.start()
    to_left.start()

    loads[0].wait()
    product = multiply(shifted, block, order[0])

    to_right.wait()
    to_left.wait()
    low = jnp.where(hours > 0, edge[0].astype(jnp.float32), blank)
    high = jnp.where(hours < n_hours - 1, edge[1].astype(jnp.float32), blank)
    turned = jnp.concatenate([low, blank, blank, high], axis=1)
    for step in range(TAPS):
        shift = (step - REACH) % turned.shape[1]
        moved = turned if shift == 0 else pltpu.roll(turned, shift, 1)
        ends[pl.ds(step * k, k), :] = moved[:, EDGE : 3 * EDGE].astype(jnp.bfloat16)
    shifted[:, pl.ds(0, EDGE)] += ends[:, pl.ds(0, EDGE)]
    shifted[:, pl.ds(width - EDGE, EDGE)] += ends[:, pl.ds(EDGE, EDGE)]
    outer = jnp.concatenate(
        [block[order[0], :, pl.ds(0, EDGE)], block[order[0], :, pl.ds(width - EDGE, EDGE)]], axis=1
    )
    product += dot_nt(ends[...], outer)

    copies = {}
    for load, mask in zip(loads, order):
        start = pl.multiple_of(flip(hours, mask) * share, share)
        if mask != order[0]:
            load.wait()
            product = multiply(shifted, block, mask)
        total = taps[pl.ds(0, 1), pl.ds(start, share)] * product[:k]
        for step in range(1, TAPS):
            total += (
                taps[pl.ds(step, 1), pl.ds(start, share)] * product[step * k : (step + 1) * k]
            )
        bit = 1
        while mask + bit < n_hours and (mask == 0 or bit < mask & -mask):
            copies[mask + bit].wait()
            arrived = recv if bit == 1 else recv_far
            total += arrived[mask + bit - 1].astype(jnp.float32)
            bit *= 2
        if mask:
            near = mask % 2 == 1
            source, target = (send, recv) if near else (send_far, recv_far)
            source[mask - 1] = total.astype(source.dtype)
            copies[mask] = pltpu.make_async_remote_copy(
                src_ref=source.at[mask - 1],
                dst_ref=target.at[mask - 1],
                send_sem=part_send.at[mask - 1],
                recv_sem=part_recv.at[mask - 1],
                device_id={"hours": flip(hours, mask & -mask)},
                device_id_type=MESH,
            )
            copies[mask].start()
    local = total
    local_out[...] = local

    gram = pack(dot_nt(local, local, HIGHEST))
    for axis, count, me, slots, send_sems, recv_sems in (
        ("hours", n_hours, hours, gram_h, gh_send, gh_recv),
        ("users", n_users, users, gram_u, gu_send, gu_recv),
    ):
        slots[me] = gram
        copies = []
        for step in range(1, count):
            copy = pltpu.make_async_remote_copy(
                src_ref=slots.at[me],
                dst_ref=slots.at[me],
                send_sem=send_sems.at[step - 1],
                recv_sem=recv_sems.at[step - 1],
                device_id={axis: (me + step) % count},
                device_id_type=MESH,
            )
            copy.start()
            copies.append(copy)
        for copy in copies:
            copy.wait()
        gram = slots[0]
        for slot in range(1, count):
            gram = gram + slots[slot]

    gram_out[...] = gram


def finish(scale, local, gram, basis, triangle):
    upper, inverse = eliminate(unpack(gram[...]))
    triangle[...] = upper * scale
    basis[...] = jnp.dot(
        inverse, local[...], precision=HIGHEST, preferred_element_type=jnp.float32
    )


def per_device(activity, cohort, tap_table, sketch):
    n_users, n_hours = lax.axis_size("users"), lax.axis_size("hours")
    rows, width = activity.shape
    k = sketch.shape[1]
    share = rows // n_hours
    dma = lambda count: pltpu.SemaphoreType.DMA((count,))
    vmem = pl.BlockSpec(memory_space=pltpu.VMEM)
    local, gram = pl.pallas_call(
        functools.partial(kernel, n_users, n_hours),
        out_shape=(
            jax.ShapeDtypeStruct((k, share), jnp.float32),
            jax.ShapeDtypeStruct((k // 2, 2 * k), jnp.float32),
        ),
        in_specs=[pl.BlockSpec(memory_space=pl.ANY), vmem, vmem, vmem],
        out_specs=(vmem, vmem),
        scratch_shapes=[
            pltpu.VMEM((n_hours, share, width), jnp.bfloat16),
            pltpu.VMEM((2, k, EDGE), jnp.bfloat16),
            pltpu.VMEM((TAPS * k, width), jnp.bfloat16),
            pltpu.VMEM((TAPS * k, 2 * EDGE), jnp.bfloat16),
            pltpu.VMEM((TAPS, rows), jnp.float32),
            pltpu.VMEM((n_hours - 1, k, share), jnp.float32),
            pltpu.VMEM((n_hours - 1, k, share), jnp.float32),
            pltpu.VMEM((n_hours - 1, k, share), jnp.bfloat16),
            pltpu.VMEM((n_hours - 1, k, share), jnp.bfloat16),
            pltpu.VMEM((n_hours, k // 2, 2 * k), jnp.float32),
            pltpu.VMEM((n_users, k // 2, 2 * k), jnp.float32),
            dma(n_hours), dma(2), dma(2),
            dma(n_hours - 1), dma(n_hours - 1),
            dma(n_hours - 1), dma(n_hours - 1),
            dma(n_users - 1), dma(n_users - 1),
        ],
        compiler_params=pltpu.CompilerParams(
            collective_id=0, has_side_effects=True, vmem_limit_bytes=56 * 1024 * 1024
        ),
        name="range_finder",
    )(activity, cohort[None, :], tap_table, sketch.T)
    basis, triangle = pl.pallas_call(
        functools.partial(finish, 1.0 / math.sqrt(rows * n_users)),
        out_shape=(
            jax.ShapeDtypeStruct((k, share), jnp.float32),
            jax.ShapeDtypeStruct((k, k), jnp.float32),
        ),
        in_specs=[vmem, vmem],
        out_specs=(vmem, vmem),
        name="factor",
    )(local, gram)
    return basis.T, triangle


def solution(mesh):
    return jax.shard_map(
        per_device,
        mesh=mesh,
        in_specs=(P(("groups", "users"), "hours"), P(("groups", "users")), P(), P("hours", None)),
        out_specs=(P(("groups", "users", "hours"), None), P("groups", None)),
        check_vma=False,
    )
```

```python
import functools
import math

import jax
import jax.numpy as jnp
from jax import lax
from jax.experimental import pallas as pl
from jax.experimental.pallas import tpu as pltpu
from jax.sharding import PartitionSpec as P

TAPS = 9
REACH = (TAPS - 1) // 2
EDGE = 128
PANEL = 8
HIGHEST = lax.Precision.HIGHEST
MESH = pl.DeviceIdType.MESH


def flip(index, mask):
    bit = 1
    while bit <= mask:
        if mask & bit:
            index = index + bit - 2 * bit * ((index // bit) % 2)
        bit *= 2
    return index


def dot_nt(a, b, precision=None):
    return lax.dot_general(
        a, b, (((1,), (1,)), ((), ())), precision=precision, preferred_element_type=jnp.float32
    )


def multiply(shifted, block, slot):
    share = block.shape[1]
    half = share // 2
    return jnp.concatenate(
        [dot_nt(shifted[...], block[slot, pl.ds(first, half), :]) for first in (0, half)], axis=1
    )


def eliminate(gram):
    k = gram.shape[0]
    row_id = lax.broadcasted_iota(jnp.int32, (k, 2 * k), 0)
    lane_id = lax.broadcasted_iota(jnp.int32, (k, 2 * k), 1)
    eye = (row_id[:, :k] == lane_id[:, :k]).astype(jnp.float32)
    work = jnp.concatenate([gram, eye], axis=1)
    diag_id = lax.broadcasted_iota(jnp.int32, (PANEL, 2 * k), 0)
    done = []
    for first in range(0, k, PANEL):
        rows = work.shape[0]
        below = lax.broadcasted_iota(jnp.int32, (rows, 2 * k), 0)
        cols = [
            jnp.broadcast_to(work[:, first + i : first + i + 1], (rows, 2 * k))
            for i in range(PANEL)
        ]
        pivots = jnp.zeros((PANEL, 2 * k), jnp.float32)
        for i in range(PANEL):
            pivot = cols[i][i : i + 1, :]
            pivots = jnp.where(diag_id == i, pivot, pivots)
            col = jnp.where(below > i, cols[i], 0.0) * (1.0 / pivot)
            for later in range(i + 1, PANEL):
                cols[later] = cols[later] - col * cols[i][later : later + 1, :]
            work = work - col * work[i : i + 1, :]
        done.append(work[:PANEL] * lax.rsqrt(pivots))
        work = work[PANEL:]
    work = jnp.concatenate(done, axis=0)
    upper = jnp.where(row_id[:, :k] <= lane_id[:, :k], work[:, :k], 0.0)
    inverse = jnp.where(row_id[:, :k] >= lane_id[:, :k], work[:, k:], 0.0)
    return upper, inverse


def pack(square):
    half = square.shape[0] // 2
    return jnp.concatenate([square[:half], square[half:]], axis=1)


def unpack(packed):
    k = packed.shape[1] // 2
    return jnp.concatenate([packed[:, :k], packed[:, k:]], axis=0)


def kernel(
    n_users, n_hours, activity, cohort, table, sketch, local_out, gram_out,
    block, edge, shifted, ends, taps, send, recv, send_far, recv_far, gram_h, gram_u,
    load_sem, edge_send, edge_recv, part_send, part_recv, gh_send, gh_recv, gu_send, gu_recv,
):
    users = lax.axis_index("users")
    hours = lax.axis_index("hours")
    rows, width = activity.shape
    k = sketch.shape[0]
    share = rows // n_hours

    order = list(range(n_hours - 1, 0, -1)) + [0]
    loads = []
    for mask in order:
        start = pl.multiple_of(flip(hours, mask) * share, share)
        load = pltpu.make_async_copy(
            activity.at[pl.ds(start, share), :], block.at[mask], load_sem.at[mask]
        )
        load.start()
        loads.append(load)

    barrier = pltpu.get_barrier_semaphore()
    for mask in range(1, n_hours):
        pl.semaphore_signal(
            barrier, inc=1, device_id={"hours": flip(hours, mask)}, device_id_type=MESH
        )
    for step in range(1, n_users):
        pl.semaphore_signal(
            barrier, inc=1, device_id={"users": (users + step) % n_users}, device_id_type=MESH
        )
    cohorts = table.shape[0]
    onehot = (
        lax.broadcasted_iota(jnp.int32, (cohorts, rows), 0) == cohort[...]
    ).astype(jnp.float32)
    taps[...] = lax.dot_general(
        table[...], onehot, (((0,), (0,)), ((), ())),
        precision=HIGHEST, preferred_element_type=jnp.float32,
    )

    middle = sketch[...].astype(jnp.float32)
    blank = jnp.zeros((k, EDGE), jnp.float32)
    turned = jnp.concatenate([blank, middle, blank], axis=1)
    for step in range(TAPS):
        shift = (step - REACH) % turned.shape[1]
        moved = turned if shift == 0 else pltpu.roll(turned, shift, 1)
        shifted[pl.ds(step * k, k), :] = moved[:, EDGE : EDGE + width].astype(jnp.bfloat16)

    pl.semaphore_wait(barrier, n_hours - 1 + n_users - 1)

    to_right = pltpu.make_async_remote_copy(
        src_ref=sketch.at[:, pl.ds(width - EDGE, EDGE)],
        dst_ref=edge.at[0],
        send_sem=edge_send.at[0],
        recv_sem=edge_recv.at[0],
        device_id={"hours": (hours + 1) % n_hours},
        device_id_type=MESH,
    )
    to_left = pltpu.make_async_remote_copy(
        src_ref=sketch.at[:, pl.ds(0, EDGE)],
        dst_ref=edge.at[1],
        send_sem=edge_send.at[1],
        recv_sem=edge_recv.at[1],
        device_id={"hours": (hours + n_hours - 1) % n_hours},
        device_id_type=MESH,
    )
    to_right.start()
    to_left.start()

    loads[0].wait()
    product = multiply(shifted, block, order[0])

    to_right.wait()
    to_left.wait()
    low = jnp.where(hours > 0, edge[0].astype(jnp.float32), blank)
    high = jnp.where(hours < n_hours - 1, edge[1].astype(jnp.float32), blank)
    turned = jnp.concatenate([low, blank, blank, high], axis=1)
    for step in range(TAPS):
        shift = (step - REACH) % turned.shape[1]
        moved = turned if shift == 0 else pltpu.roll(turned, shift, 1)
        ends[pl.ds(step * k, k), :] = moved[:, EDGE : 3 * EDGE].astype(jnp.bfloat16)
    shifted[:, pl.ds(0, EDGE)] += ends[:, pl.ds(0, EDGE)]
    shifted[:, pl.ds(width - EDGE, EDGE)] += ends[:, pl.ds(EDGE, EDGE)]
    outer = jnp.concatenate(
        [block[order[0], :, pl.ds(0, EDGE)], block[order[0], :, pl.ds(width - EDGE, EDGE)]], axis=1
    )
    product += dot_nt(ends[...], outer)

    copies = {}
    for load, mask in zip(loads, order):
        start = pl.multiple_of(flip(hours, mask) * share, share)
        if mask != order[0]:
            load.wait()
            product = multiply(shifted, block, mask)
        total = taps[pl.ds(0, 1), pl.ds(start, share)] * product[:k]
        for step in range(1, TAPS):
            total += (
                taps[pl.ds(step, 1), pl.ds(start, share)] * product[step * k : (step + 1) * k]
            )
        bit = 1
        while mask + bit < n_hours and (mask == 0 or bit < mask & -mask):
            copies[mask + bit].wait()
            arrived = recv if bit == 1 else recv_far
            total += arrived[mask + bit - 1].astype(jnp.float32)
            bit *= 2
        if mask:
            near = mask % 2 == 1
            source, target = (send, recv) if near else (send_far, recv_far)
            source[mask - 1] = total.astype(source.dtype)
            copies[mask] = pltpu.make_async_remote_copy(
                src_ref=source.at[mask - 1],
                dst_ref=target.at[mask - 1],
                send_sem=part_send.at[mask - 1],
                recv_sem=part_recv.at[mask - 1],
                device_id={"hours": flip(hours, mask & -mask)},
                device_id_type=MESH,
            )
            copies[mask].start()
    local = total
    local_out[...] = local

    gram = pack(dot_nt(local, local, HIGHEST))
    for axis, count, me, slots, send_sems, recv_sems in (
        ("hours", n_hours, hours, gram_h, gh_send, gh_recv),
        ("users", n_users, users, gram_u, gu_send, gu_recv),
    ):
        slots[me] = gram
        copies = []
        for step in range(1, count):
            copy = pltpu.make_async_remote_copy(
                src_ref=slots.at[me],
                dst_ref=slots.at[me],
                send_sem=send_sems.at[step - 1],
                recv_sem=recv_sems.at[step - 1],
                device_id={axis: (me + step) % count},
                device_id_type=MESH,
            )
            copy.start()
            copies.append(copy)
        for copy in copies:
            copy.wait()
        gram = slots[0]
        for slot in range(1, count):
            gram = gram + slots[slot]

    gram_out[...] = gram


def finish(scale, local, gram, basis, triangle):
    upper, inverse = eliminate(unpack(gram[...]))
    triangle[...] = upper * scale
    high = inverse.astype(jnp.bfloat16)
    rest = (inverse - high.astype(jnp.float32)).astype(jnp.bfloat16)
    values = local[...]
    main = values.astype(jnp.bfloat16)
    minor = (values - main.astype(jnp.float32)).astype(jnp.bfloat16)
    basis[...] = jnp.dot(
        jnp.concatenate([high, rest, high], axis=1),
        jnp.concatenate([main, main, minor], axis=0),
        preferred_element_type=jnp.float32,
    )


def per_device(activity, cohort, tap_table, sketch):
    n_users, n_hours = lax.axis_size("users"), lax.axis_size("hours")
    rows, width = activity.shape
    k = sketch.shape[1]
    share = rows // n_hours
    dma = lambda count: pltpu.SemaphoreType.DMA((count,))
    vmem = pl.BlockSpec(memory_space=pltpu.VMEM)
    local, gram = pl.pallas_call(
        functools.partial(kernel, n_users, n_hours),
        out_shape=(
            jax.ShapeDtypeStruct((k, share), jnp.float32),
            jax.ShapeDtypeStruct((k // 2, 2 * k), jnp.float32),
        ),
        in_specs=[pl.BlockSpec(memory_space=pl.ANY), vmem, vmem, vmem],
        out_specs=(vmem, vmem),
        scratch_shapes=[
            pltpu.VMEM((n_hours, share, width), jnp.bfloat16),
            pltpu.VMEM((2, k, EDGE), jnp.bfloat16),
            pltpu.VMEM((TAPS * k, width), jnp.bfloat16),
            pltpu.VMEM((TAPS * k, 2 * EDGE), jnp.bfloat16),
            pltpu.VMEM((TAPS, rows), jnp.float32),
            pltpu.VMEM((n_hours - 1, k, share), jnp.float32),
            pltpu.VMEM((n_hours - 1, k, share), jnp.float32),
            pltpu.VMEM((n_hours - 1, k, share), jnp.bfloat16),
            pltpu.VMEM((n_hours - 1, k, share), jnp.bfloat16),
            pltpu.VMEM((n_hours, k // 2, 2 * k), jnp.float32),
            pltpu.VMEM((n_users, k // 2, 2 * k), jnp.float32),
            dma(n_hours), dma(2), dma(2),
            dma(n_hours - 1), dma(n_hours - 1),
            dma(n_hours - 1), dma(n_hours - 1),
            dma(n_users - 1), dma(n_users - 1),
        ],
        compiler_params=pltpu.CompilerParams(
            collective_id=0, has_side_effects=True, vmem_limit_bytes=56 * 1024 * 1024
        ),
        name="range_finder",
    )(activity, cohort[None, :], tap_table, sketch.T)
    basis, triangle = pl.pallas_call(
        functools.partial(finish, 1.0 / math.sqrt(rows * n_users)),
        out_shape=(
            jax.ShapeDtypeStruct((k, share), jnp.float32),
            jax.ShapeDtypeStruct((k, k), jnp.float32),
        ),
        in_specs=[vmem, vmem],
        out_specs=(vmem, vmem),
        name="factor",
    )(local, gram)
    return basis.T, triangle


def solution(mesh):
    return jax.shard_map(
        per_device,
        mesh=mesh,
        in_specs=(P(("groups", "users"), "hours"), P(("groups", "users")), P(), P("hours", None)),
        out_specs=(P(("groups", "users", "hours"), None), P("groups", None)),
        check_vma=False,
    )
```
